32 devices in a mesh: dp: 8 (over y, x, core), expert: 4 (over z).
Axes of the slice: x: 2, y: 2, z: 4, core: 2. Of those that a mesh axis runs over, the one named last changes fastest.
Arguments:
- layer_input: bfloat16 [4096, 2560], P(('dp', 'expert')), may hold values from -6 to 6
- output_grad: bfloat16 [4096, 2560], P(('dp', 'expert')), may hold values from -6 to 6
- expert_ids: int32 [4096, 2], P(('dp', 'expert')), may hold values from 0 to 3, all different within a row; in each aligned block of 128 rows (0 to 127, 128 to 255, ...) at most 96 rows name the same one
- gate_probs: bfloat16 [4096, 2], P(('dp', 'expert')), may hold values from 0.099609375 to 0.59765625
- gate_weight: float32 [4, 2560, 1536], P('expert', 'dp'), may hold values from -0.125 to 0.125
- up_weight: float32 [4, 2560, 1536], P('expert', 'dp'), may hold values from -0.125 to 0.125
- down_weight: float32 [4, 1536, 2560], P('expert', 'dp'), may hold values from -0.15625 to 0.15625
- gate_moment: float32 [4, 2560, 1536], P('expert', 'dp'), may hold values from -12 to 12
- up_moment: float32 [4, 2560, 1536], P('expert', 'dp'), may hold values from -12 to 12
- down_moment: float32 [4, 1536, 2560], P('expert', 'dp'), may hold values from -12 to 12
- gate_second: float32 [4, 2560, 1536], P('expert', 'dp'), may hold values from 1 to 100
- up_second: float32 [4, 2560, 1536], P('expert', 'dp'), may hold values from 1 to 100
- down_second: float32 [4, 1536, 2560], P('expert', 'dp'), may hold values from 1 to 100
Outputs:
- input_grad: bfloat16 [4096, 2560], P(('dp', 'expert'))
- prob_grad: bfloat16 [4096, 2], P(('dp', 'expert'))
- new_gate_weight: float32 [4, 2560, 1536], P('expert', 'dp')
- new_up_weight: float32 [4, 2560, 1536], P('expert', 'dp')
- new_down_weight: float32 [4, 1536, 2560], P('expert', 'dp')
- new_gate_moment: float32 [4, 2560, 1536], P('expert', 'dp')
- new_up_moment: float32 [4, 2560, 1536], P('expert', 'dp')
- new_down_moment: float32 [4, 1536, 2560], P('expert', 'dp')
- new_gate_second: float32 [4, 2560, 1536], P('expert', 'dp')
- new_up_second: float32 [4, 2560, 1536], P('expert', 'dp')
- new_down_second: float32 [4, 1536, 2560], P('expert', 'dp')
The draws below stay inside these ranges and needn't reach their ends.
Inputs may be any that keep to these rules, and one draw needn't show every extreme that they name: `expert_ids`: each token names 2 different experts. Among the (token, pick) pairs of one device's 128 tokens, no expert is named more than 96 times, and in every draw some device's tokens name some expert exactly 96 times.
All inputs are finite; a program needn't handle non-finite values.
Results may differ from the reference program's by a relative error of at most 0.025.
Values may be sent and summed in bfloat16 or wider, within the bound.
A program may use at most 256 MiB of HBM per device.

```python
import math
import jax
import jax.numpy as jnp
import numpy as np
from jax import lax

D = 2560
FF = 1536
EXP_DEV = 1
PICKS = 2
TOK_DEV = 128
EXPERTS = 4
CAP = 96
TOKENS = 4096
N_DP = 8
N_EXPERT = 4


def levels(own_key, shape, shards, low, top_value):
    def one(dim, shards_of):
        steps = jax.random.uniform(jax.random.fold_in(jax.random.fold_in(own_key, 6), dim), (shards_of,), jnp.float32, low / len(shards), top_value / len(shards))
        return jnp.repeat(jnp.exp(steps), shape[dim] // shards_of).reshape((-1,) + (1,) * (len(shape) - dim - 1))

    gain = one(*shards[0])
    for cut in shards[1:]:
        gain = gain * one(*cut)
    return gain


def shared_out(key, own, number, rows, number_of, top, most, lean):
    order = jax.random.permutation(key, number_of)
    heavy_load, usual = portions_of(number_of, rows * top, most, lean, True), portions_of(number_of, rows * top, most, lean, False)
    places = jnp.arange(number_of)

    def named(lengths, rotation):
        used = int((lengths > 0).sum())
        fixed = max(1, used // 4)
        shifted = fixed + (places - fixed + rotation * (used - fixed)) % max(1, number_of - fixed)
        return jnp.zeros((number_of,), jnp.int32).at[order[jnp.where(places < fixed, places, shifted)]].set(jnp.asarray(lengths, jnp.int32))

    lengths = jnp.where(number % 4 == 0, named(heavy_load, number // 4), named(usual, number - number // 4 - 1))
    mixed = jax.random.permutation(jax.random.fold_in(own, 3), number_of)
    giver, taker = mixed[0:number_of // 2 * 2:2], mixed[1:number_of // 2 * 2:2]
    room = jnp.minimum(lengths[giver] - 1, most - lengths[taker]) // 2
    room = jnp.where((giver == order[0]) | (taker == order[0]) | (lengths[taker] == 0), 0, jnp.maximum(room, 0))
    shifted = jax.random.randint(jax.random.fold_in(own, 4), (number_of // 2,), 0, 1 << 20) % (room + 1)
    lengths = lengths.at[giver].add(-shifted).at[taker].add(shifted)
    labels = jnp.searchsorted(jnp.cumsum(lengths), jnp.arange(rows * top), side="right").astype(jnp.int32)
    grid = labels.reshape(top, rows).T
    grid = grid[jax.random.permutation(jax.random.fold_in(own, 1), rows)]
    rotation = jax.random.randint(jax.random.fold_in(own, 2), (rows, 1), 0, top)
    return jnp.take_along_axis(grid, (jnp.arange(top)[None, :] + rotation) % top, axis=1)


def portions_of(count, total, most, skew, full):
    weights = [(1 << 20) // math.isqrt(standing ** skew) + 1 for standing in range(1, count + 1)]
    largest = most if full else min(most, max(-(-total // count), total * weights[0] // sum(weights)))
    least = 1 if total - largest >= count - 1 else 0
    holding, surplus = [largest] + [least] * (count - 1), total - largest - least * (count - 1)
    while surplus > 0:
        free = [i for i in range(1, count) if holding[i] < largest] or [i for i in range(1, count) if holding[i] < most]
        mass, budget = sum([weights[i] for i in free]), surplus
        for i in free:
            extra = min(most - holding[i], max(1, budget * weights[i] // mass), surplus)
            holding[i] = holding[i] + extra
            surplus = surplus - extra
    return np.array(holding)


def noise(own_key, extent, width, most, pieces=(), held_as=jnp.bfloat16):
    drawn = jax.random.normal(own_key, extent, jnp.float32) * width
    if len(pieces) > 0:
        drawn = levels(own_key, extent, pieces, -0.22, 0.18) * drawn
    return jnp.clip(drawn, min=-most, max=most).astype(held_as)


def setup_inputs(seed: int = 0) -> dict:
    seeds = jax.random.split(jax.random.key(seed), 14)
    layer_input = noise(seeds[0], (TOKENS, D), 1.0, 6.0, ((0, 32),))
    output_grad = noise(seeds[1], (TOKENS, D), 1.0, 6.0, ((0, 32),))
    expert_ids_keys = jax.random.split(jax.random.fold_in(seeds[2], 1), TOKENS // TOK_DEV)
    expert_ids_turns = jax.random.permutation(jax.random.fold_in(seeds[2], 3), TOKENS // TOK_DEV)
    expert_ids = jax.vmap(lambda own, number: shared_out(jax.random.fold_in(seeds[2], 2), own, number, TOK_DEV, EXPERTS, PICKS, CAP, 2))(expert_ids_keys, expert_ids_turns).reshape((TOKENS, PICKS))
    gate_probs = jnp.clip(0.099609375 + 0.49804688 * jax.random.uniform(seeds[3], (TOKENS, PICKS), jnp.float32) ** levels(seeds[3], (TOKENS, PICKS), ((0, 32),), -0.2, 0.2), 0.099609375, 0.59765625).astype(jnp.bfloat16)
    gate_weight = noise(seeds[4], (EXPERTS, D, FF), D ** -0.5, 0.125, ((0, 4), (1, 8)), jnp.float32)
    up_weight = noise(seeds[5], (EXPERTS, D, FF), D ** -0.5, 0.125, ((0, 4), (1, 8)), jnp.float32)
    down_weight = noise(seeds[6], (EXPERTS, FF, D), FF ** -0.5, 0.15625, ((0, 4), (1, 8)), jnp.float32)
    gate_moment = noise(seeds[7], (EXPERTS, D, FF), 2.0, 12.0, ((0, 4), (1, 8)), jnp.float32)
    up_moment = noise(seeds[8], (EXPERTS, D, FF), 2.0, 12.0, ((0, 4), (1, 8)), jnp.float32)
    down_moment = noise(seeds[9], (EXPERTS, FF, D), 2.0, 12.0, ((0, 4), (1, 8)), jnp.float32)
    gate_second = jnp.clip(jnp.exp(math.log(100.0) - 4.6051702 * jax.random.uniform(seeds[10], (EXPERTS, D, FF), jnp.float32) ** levels(seeds[10], (EXPERTS, D, FF), ((0, 4), (1, 8)), -0.2, 0.2)), 1.0, 100.0)
    up_second = jnp.clip(jnp.exp(math.log(100.0) - 4.6051702 * jax.random.uniform(seeds[11], (EXPERTS, D, FF), jnp.float32) ** levels(seeds[11], (EXPERTS, D, FF), ((0, 4), (1, 8)), -0.2, 0.2)), 1.0, 100.0)
    down_second = jnp.clip(jnp.exp(math.log(100.0) - 4.6051702 * jax.random.uniform(seeds[12], (EXPERTS, FF, D), jnp.float32) ** levels(seeds[12], (EXPERTS, FF, D), ((0, 4), (1, 8)), -0.2, 0.2)), 1.0, 100.0)
    return {"layer_input": layer_input, "output_grad": output_grad, "expert_ids": expert_ids, "gate_probs": gate_probs, "gate_weight": gate_weight, "up_weight": up_weight, "down_weight": down_weight, "gate_moment": gate_moment, "up_moment": up_moment, "down_moment": down_moment, "gate_second": gate_second, "up_second": up_second, "down_second": down_second}


beta_one = 0.9
beta_two = 0.95
learn_rate = 0.003
decay_rate = 0.1
epsilon = 1e-08
correct_one = 1.0 - 2.6561398887587e-05
correct_two = 1.0 - 0.005920529220333

def slot_tables(flat_ids, expert_count, exp_dev, groups, capacity):
    onehot = (flat_ids[:, None] == jnp.arange(expert_count, dtype=jnp.int32)[None, :]).astype(jnp.int32)
    before = jnp.cumsum(onehot, axis=0) - onehot
    ranked = lax.optimization_barrier(jnp.sum(before * onehot, axis=1)).astype(jnp.int32)
    device = flat_ids // exp_dev
    local = flat_ids % exp_dev
    return ((local * groups + device) * capacity + ranked).astype(jnp.int32)

def build_rows(dest_slot, inputs, grads, probs):
    slots = EXPERTS * CAP
    owner = jnp.zeros((slots,), jnp.int32).at[dest_slot].set(jnp.arange(TOK_DEV * PICKS, dtype=jnp.int32) // PICKS)
    filled = jnp.zeros((slots,), jnp.int32).at[dest_slot].set(1) > 0
    zero_val = jnp.zeros((), inputs.dtype)
    send_input = jnp.where(filled[:, None], inputs[owner], zero_val)
    send_grad = jnp.where(filled[:, None], grads[owner], zero_val)
    send_gate = jnp.zeros((slots,), probs.dtype).at[dest_slot].set(probs.reshape(-1))
    return (send_input, send_grad, send_gate)

def expert_backward(args):
    x_rows, dy_rows, gate_rows, w_gate_up, w_down = args
    pre = jnp.dot(x_rows, w_gate_up, preferred_element_type=jnp.float32)
    gate_pre = pre[:, :FF]
    up_pre = pre[:, FF:]
    sigmoid_gate = jax.nn.sigmoid(gate_pre)
    silu_gate = gate_pre * sigmoid_gate
    hidden = (silu_gate * up_pre).astype(jnp.bfloat16)
    expert_out = jnp.dot(hidden, w_down, preferred_element_type=jnp.float32)
    prob_rows = lax.optimization_barrier(jnp.sum(dy_rows.astype(jnp.float32) * expert_out, axis=1)).astype(jnp.bfloat16)
    out_scaled = (gate_rows.astype(jnp.float32)[:, None] * dy_rows.astype(jnp.float32)).astype(jnp.bfloat16)
    hidden_grad = jnp.dot(out_scaled, w_down.T, preferred_element_type=jnp.float32)
    dsilu = sigmoid_gate * (1.0 + gate_pre * (1.0 - sigmoid_gate))
    pre_grad = jnp.concatenate((hidden_grad * up_pre * dsilu, hidden_grad * silu_gate), axis=1).astype(jnp.bfloat16)
    input_rows = jnp.dot(pre_grad, w_gate_up.T, preferred_element_type=jnp.float32).astype(jnp.bfloat16)
    term_gate_up = jnp.dot(x_rows.T, pre_grad, preferred_element_type=jnp.float32)
    term_down = jnp.dot(hidden.T, out_scaled, preferred_element_type=jnp.float32)
    return (input_rows, prob_rows, term_gate_up, term_down)

def adamw(weight, moment, second, grad):
    moment_new = beta_one * moment + (1.0 - beta_one) * grad
    second_new = beta_two * second + (1.0 - beta_two) * grad * grad
    update = moment_new / correct_one / (jnp.sqrt(second_new / correct_two) + epsilon)
    return (weight - learn_rate * (update + decay_rate * weight), moment_new, second_new)

def rounded(value):
    return lax.optimization_barrier(value.astype(jnp.bfloat16)).astype(jnp.float32)

def reference(layer_input, output_grad, expert_ids, gate_probs, gate_weight, up_weight, down_weight, gate_moment, up_moment, down_moment, gate_second, up_second, down_second):
    devices = N_DP * N_EXPERT
    rows = N_EXPERT * CAP
    flat_ids = expert_ids.reshape(devices, TOK_DEV * PICKS)
    dest_slot = jax.vmap(lambda ids: slot_tables(ids, EXPERTS, EXP_DEV, N_EXPERT, CAP))(flat_ids)
    send_input, send_grad, send_gate = jax.vmap(build_rows)(dest_slot, layer_input.reshape(devices, TOK_DEV, D), output_grad.reshape(devices, TOK_DEV, D), gate_probs.reshape(devices, TOK_DEV, PICKS))

    def regroup(buffer):
        shaped = buffer.reshape((N_DP, N_EXPERT, EXP_DEV, N_EXPERT, CAP) + buffer.shape[2:])
        order = (0, 3, 2, 1, 4) + tuple(range(5, shaped.ndim))
        return jnp.transpose(shaped, order).reshape((N_DP, EXPERTS, rows) + buffer.shape[2:])
    x_all = regroup(send_input)
    dy_all = regroup(send_grad)
    gate_all = regroup(send_gate)
    w_gate_up = jnp.concatenate((gate_weight, up_weight), axis=2).astype(jnp.bfloat16)
    w_down = down_weight.astype(jnp.bfloat16)

    def per_group(carry, piece):
        acc_gate_up, acc_down = carry
        x_rows, dy_rows, gate_rows = piece
        input_rows, prob_rows, term_gate_up, term_down = lax.map(expert_backward, (x_rows, dy_rows, gate_rows, w_gate_up, w_down))
        return ((acc_gate_up + rounded(term_gate_up), acc_down + rounded(term_down)), (input_rows, prob_rows))
    init = (jnp.zeros((EXPERTS, D, 2 * FF), jnp.float32), jnp.zeros((EXPERTS, FF, D), jnp.float32))
    (grad_gate_up, grad_down), (input_rows, prob_rows) = lax.scan(per_group, init, (x_all, dy_all, gate_all))

    def ungroup(buffer):
        shaped = buffer.reshape((N_DP, N_EXPERT, EXP_DEV, N_EXPERT, CAP) + buffer.shape[3:])
        order = (0, 3, 2, 1, 4) + tuple(range(5, shaped.ndim))
        return jnp.transpose(shaped, order).reshape((devices, EXPERTS * CAP) + buffer.shape[3:])
    back_rows = jax.vmap(lambda table, dest: table[dest])(ungroup(input_rows), dest_slot)
    input_grad = lax.optimization_barrier(jnp.sum(back_rows.reshape(devices, TOK_DEV, PICKS, D).astype(jnp.float32), axis=2)).astype(jnp.bfloat16).reshape(TOKENS, D)
    back_probs = jax.vmap(lambda table, dest: table[dest])(ungroup(prob_rows), dest_slot)
    prob_grad = back_probs.reshape(TOKENS, PICKS)
    new_gate_weight, new_gate_moment, new_gate_second = adamw(gate_weight, gate_moment, gate_second, grad_gate_up[:, :, :FF])
    new_up_weight, new_up_moment, new_up_second = adamw(up_weight, up_moment, up_second, grad_gate_up[:, :, FF:])
    new_down_weight, new_down_moment, new_down_second = adamw(down_weight, down_moment, down_second, grad_down)
    return (input_grad, prob_grad, new_gate_weight, new_up_weight, new_down_weight, new_gate_moment, new_up_moment, new_down_moment, new_gate_second, new_up_second, new_down_second)
```

```python
import functools

import jax
import jax.numpy as jnp
from jax import lax
from jax.experimental import pallas as pl
from jax.experimental.pallas import tpu as pltpu
from jax.sharding import PartitionSpec as P

beta_one = 0.9
beta_two = 0.95
learn_rate = 0.003
decay_rate = 0.1
epsilon = 1e-08
correct_one = 1.0 - 2.6561398887587e-05
correct_two = 1.0 - 0.005920529220333


def slot_tables(flat_ids, expert_count, exp_dev, groups, capacity):
    onehot = (flat_ids[:, None] == jnp.arange(expert_count, dtype=jnp.int32)[None, :]).astype(
        jnp.int32
    )
    before = jnp.cumsum(onehot, axis=0) - onehot
    ranked = jnp.sum(before * onehot, axis=1)
    device = flat_ids // exp_dev
    local = flat_ids % exp_dev
    return (local * groups + device) * capacity + ranked


def adamw(weight, moment, second, grad):
    moment_new = beta_one * moment + (1.0 - beta_one) * grad
    second_new = beta_two * second + (1.0 - beta_two) * grad * grad
    update = moment_new / correct_one / (jnp.sqrt(second_new / correct_two) + epsilon)
    return (weight - learn_rate * (update + decay_rate * weight), moment_new, second_new)


def body(
    layer_input,
    output_grad,
    expert_ids,
    gate_probs,
    gate_weight,
    up_weight,
    down_weight,
    gate_moment,
    up_moment,
    down_moment,
    gate_second,
    up_second,
    down_second,
):
    exp_dev = gate_weight.shape[0]
    hidden_units = gate_weight.shape[2]
    width = layer_input.shape[1]
    groups = lax.axis_size("expert")
    shards = lax.axis_size("dp")
    tok_count, picks = expert_ids.shape
    capacity = 3 * tok_count * picks // (2 * exp_dev * groups)
    slots = exp_dev * groups * capacity
    row_count = groups * capacity
    dest_slot = slot_tables(expert_ids.reshape(-1), exp_dev * groups, exp_dev, groups, capacity)
    owner = (
        jnp.zeros((slots,), jnp.int32)
        .at[dest_slot]
        .set(jnp.arange(tok_count * picks, dtype=jnp.int32) // picks)
    )
    filled = jnp.zeros((slots,), jnp.int32).at[dest_slot].set(1) > 0
    zero_val = jnp.zeros((), jnp.bfloat16)
    send_input = jnp.where(filled[:, None], layer_input[owner], zero_val).reshape(
        exp_dev, groups, capacity, width
    )
    send_grad = jnp.where(filled[:, None], output_grad[owner], zero_val).reshape(
        exp_dev, groups, capacity, width
    )
    send_gate = (
        jnp.zeros((slots,), jnp.bfloat16)
        .at[dest_slot]
        .set(gate_probs.reshape(-1))
        .reshape(exp_dev, groups, capacity)
    )
    w_gate_up_shard = jnp.concatenate((gate_weight, up_weight), axis=2).astype(jnp.bfloat16)
    w_down_shard = down_weight.astype(jnp.bfloat16)
    w_gate_up, w_down = (
        lax.all_gather(w_gate_up_shard, "dp", axis=1, tiled=True),
        lax.all_gather(w_down_shard, "dp", axis=1, tiled=True),
    )
    recv_input, recv_grad, recv_gate = (
        lax.all_to_all(send_input, "expert", split_axis=1, concat_axis=1, tiled=True),
        lax.all_to_all(send_grad, "expert", split_axis=1, concat_axis=1, tiled=True),
        lax.all_to_all(send_gate, "expert", split_axis=1, concat_axis=1, tiled=True),
    )
    x_rows = recv_input.reshape(exp_dev, row_count, width)
    dy_rows = recv_grad.reshape(exp_dev, row_count, width)
    gate_rows = recv_gate.reshape(exp_dev, row_count)
    pre = jnp.einsum("erd,edf->erf", x_rows, w_gate_up, preferred_element_type=jnp.float32)
    gate_pre = pre[:, :, :hidden_units]
    up_pre = pre[:, :, hidden_units:]
    sigmoid_gate = jax.nn.sigmoid(gate_pre)
    silu_gate = gate_pre * sigmoid_gate
    hidden = (silu_gate * up_pre).astype(jnp.bfloat16)
    expert_out = jnp.einsum("erf,efd->erd", hidden, w_down, preferred_element_type=jnp.float32)
    prob_rows = jnp.sum(dy_rows.astype(jnp.float32) * expert_out, axis=2).astype(jnp.bfloat16)
    out_scaled = (gate_rows.astype(jnp.float32)[:, :, None] * dy_rows.astype(jnp.float32)).astype(
        jnp.bfloat16
    )
    down_cols = hidden_units // shards
    model_cols = width // shards
    hidden_grad = jnp.einsum("erd,efd->erf", out_scaled, w_down, preferred_element_type=jnp.float32)
    dsilu = sigmoid_gate * (1.0 + gate_pre * (1.0 - sigmoid_gate))
    pre_grad = jnp.concatenate(
        (hidden_grad * up_pre * dsilu, hidden_grad * silu_gate), axis=2
    ).astype(jnp.bfloat16)
    input_rows = jnp.einsum(
        "erf,edf->erd", pre_grad, w_gate_up, preferred_element_type=jnp.float32
    ).astype(jnp.bfloat16)
    cols = x_rows
    first = jnp.einsum("erc,erf->cef", cols, pre_grad, preferred_element_type=jnp.float32).reshape(
        1 * lax.axis_size("dp"), model_cols * exp_dev * 2 * hidden_units
    )
    cols = hidden
    second = jnp.einsum(
        "erc,erd->ced", cols, out_scaled, preferred_element_type=jnp.float32
    ).reshape(1 * lax.axis_size("dp"), down_cols * exp_dev * width)
    joined = lax.psum_scatter(
        jnp.concatenate((first, second), axis=1).astype(jnp.bfloat16),
        "dp",
        scatter_dimension=0,
        tiled=True,
    ).astype(jnp.float32)
    split_at = model_cols * exp_dev * 2 * hidden_units
    grad_gate_up = joined[0, :split_at].reshape(model_cols, exp_dev, 2 * hidden_units)
    grad_down = joined[0, split_at:].reshape(down_cols, exp_dev, width)
    back_input, back_prob = (
        lax.all_to_all(
            input_rows.reshape(exp_dev, groups, capacity, width),
            "expert",
            split_axis=1,
            concat_axis=1,
            tiled=True,
        ),
        lax.all_to_all(
            prob_rows.reshape(exp_dev, groups, capacity),
            "expert",
            split_axis=1,
            concat_axis=1,
            tiled=True,
        ),
    )
    picked_rows = back_input.reshape(slots, width)[dest_slot].reshape(tok_count, picks, width)
    input_grad = jnp.sum(picked_rows.astype(jnp.float32), axis=1).astype(jnp.bfloat16)
    prob_grad = back_prob.reshape(slots)[dest_slot].reshape(tok_count, picks)
    grad_gate_up = jnp.transpose(grad_gate_up, (1, 0, 2))
    grad_down = jnp.transpose(grad_down, (1, 0, 2))
    new_gate_weight, new_gate_moment, new_gate_second = adamw(
        gate_weight, gate_moment, gate_second, grad_gate_up[:, :, :hidden_units]
    )
    new_up_weight, new_up_moment, new_up_second = adamw(
        up_weight, up_moment, up_second, grad_gate_up[:, :, hidden_units:]
    )
    new_down_weight, new_down_moment, new_down_second = adamw(
        down_weight, down_moment, down_second, grad_down
    )
    return (
        input_grad,
        prob_grad,
        new_gate_weight,
        new_up_weight,
        new_down_weight,
        new_gate_moment,
        new_up_moment,
        new_down_moment,
        new_gate_second,
        new_up_second,
        new_down_second,
    )


MESH = pl.DeviceIdType.MESH
A_PIECES, B_PIECES = (0, 1, 2), (3, 4, 5)


def place():
    me = lax.axis_index("dp")
    z = lax.axis_index("expert")
    core, col, row = me % 2, (me // 2) % 2, me // 4
    sib = me + 1 - 2 * core
    return me, z, sib, 2 - 4 * col, 4 - 8 * row


def enter(me, z, depth, peers, others):
    barrier = pltpu.get_barrier_semaphore()
    for peer in peers:
        pl.semaphore_signal(barrier, inc=1, device_id=(peer, z), device_id_type=MESH)
    for other in others:
        pl.semaphore_signal(barrier, inc=1, device_id=(me, other), device_id_type=MESH)
    pl.semaphore_wait(barrier, len(peers) + len(others))


def remote(src, dst, send, recv, device):
    return pltpu.make_async_remote_copy(
        src_ref=src, dst_ref=dst, send_sem=send, recv_sem=recv, device_id=device, device_id_type=MESH
    )


def piece_at(k, joined, down, block, rows, down_rows, hidden):
    half, part = k // 3, k % 3
    if part == 2:
        n = down_rows // 2
        return down.at[pl.ds(pl.multiple_of(block * down_rows + half * n, 16), n)]
    n = rows // 2
    return joined.at[
        pl.ds(pl.multiple_of(block * rows + part * n, 16), n), pl.ds(half * hidden, hidden)
    ]


def gather_kernel(
    depth, x, y, gm, wgu, wd, out_wgu, out_wd, out_x, out_y, out_gm, ssem, rsem, zsend, zrecv, lsem
):
    me, z, sib, dx, dy = place()
    rows, hidden, down_rows, toks = wgu.shape[0], wgu.shape[1] // 2, wd.shape[0], x.shape[0]
    enter(me, z, depth, (sib, me + dx, me + dy), ((z + 1) % depth, (z + depth - 1) % depth))

    def own(k):
        return piece_at(k, wgu, wd, 0, rows, down_rows, hidden)

    def at(k, block):
        return piece_at(k, out_wgu, out_wd, block, rows, down_rows, hidden)

    sends = []

    def send(src, k, block, kind, rel, peer):
        copy = remote(src, at(k, block), ssem.at[kind, k], rsem.at[rel, k], (peer, z))
        copy.start()
        sends.append(copy)

    def arrived(k, block, rel):
        remote(at(k, block), at(k, block), ssem.at[0, k], rsem.at[rel, k], (sib, z)).wait_recv()

    ins, outs = (x, y, gm), (out_x, out_y, out_gm)

    def zat(k, block):
        return outs[k].at[pl.ds(pl.multiple_of(block * toks, 16), toks)]

    def zcopy(way, d, k):
        sign = 1 - 2 * way
        block = z - sign * (d - 1)
        src = ins[k] if d == 1 else zat(k, block)
        return remote(src, zat(k, block), zsend.at[way, d - 1, k], zrecv.at[way, d - 1, k], (me, z + sign))

    def zwait(way, d, k):
        block = z - (1 - 2 * way) * d
        remote(
            zat(k, block), zat(k, block), zsend.at[way, d - 1, k], zrecv.at[way, d - 1, k], (me, (z + 1) % depth)
        ).wait_recv()

    def hop(d, k):
        @pl.when(z >= d)
        def _():
            zwait(0, d, k)
            if d < depth - 1:

                @pl.when(z < depth - 1)
                def _():
                    zcopy(0, d + 1, k).start()

        @pl.when(z + d <= depth - 1)
        def _():
            zwait(1, d, k)
            if d < depth - 1:

                @pl.when(z > 0)
                def _():
                    zcopy(1, d + 1, k).start()

    for i in range(3):
        send(own(A_PIECES[i]), A_PIECES[i], me, 0, 2, me + dx)
        send(own(B_PIECES[i]), B_PIECES[i], me, 1, 4, me + dy)

    @pl.when(z < depth - 1)
    def _():
        for k in (2, 0, 1):
            zcopy(0, 1, k).start()

    @pl.when(z > 0)
    def _():
        for k in (2, 0, 1):
            zcopy(1, 1, k).start()

    for i in range(3):
        send(own(B_PIECES[i]), B_PIECES[i], me, 0, 2, me + dx)
        send(own(A_PIECES[i]), A_PIECES[i], me, 1, 4, me + dy)
    for k in range(6):
        send(own(k), k, me, 2, 1, sib)
    local = [pltpu.make_async_copy(own(k), at(k, me), lsem.at[k]) for k in range(6)]
    local += [pltpu.make_async_copy(ins[k], zat(k, z), lsem.at[6 + k]) for k in range(3)]
    for copy in local:
        copy.start()

    for i in range(3):
        ka, kb = A_PIECES[i], B_PIECES[i]
        arrived(ka, me + dx, 2)
        send(at(ka, me + dx), ka, me + dx, 3, 6, me + dy)
        send(at(ka, me + dx), ka, me + dx, 4, 3, sib)
        arrived(kb, me + dy, 4)
        send(at(kb, me + dy), kb, me + dy, 3, 6, me + dx)
        send(at(kb, me + dy), kb, me + dy, 5, 5, sib)
        if i == 0:
            hop(1, 2)
        if i == 1:
            hop(1, 0)
    hop(1, 1)
    hop(2, 2)
    for i in range(3):
        ka, kb = A_PIECES[i], B_PIECES[i]
        arrived(kb, me + dx, 2)
        send(at(kb, me + dx), kb, me + dx, 4, 3, sib)
        arrived(ka, me + dy, 4)
        send(at(ka, me + dy), ka, me + dy, 5, 5, sib)
        if i == 1:
            hop(2, 0)
    hop(2, 1)
    for k in (0, 3, 1, 4, 2, 5):
        arrived(k, me + dx + dy, 6)
        send(at(k, me + dx + dy), k, me + dx + dy, 6, 7, sib)
    for k in (2, 0, 1):
        hop(3, k)
    for k in range(6):
        arrived(k, sib, 1)
        arrived(k, sib + dx, 3)
        arrived(k, sib + dy, 5)
        arrived(k, sib + dx + dy, 7)
    for copy in sends:
        copy.wait_send()
    for copy in local:
        copy.wait()
    for d in range(1, depth):
        for k in range(3):

            @pl.when((z < depth - 1) & (z >= d - 1))
            def _():
                zcopy(0, d, k).wait_send()

            @pl.when((z > 0) & (z + d - 1 <= depth - 1))
            def _():
                zcopy(1, d, k).wait_send()


def scatter_kernel(
    depth,
    p13,
    p2,
    xr,
    q,
    g13,
    g2,
    out_x,
    out_q,
    own_w,
    own_d,
    sib_w,
    sib_d,
    hop_w,
    hop_d,
    s_send,
    s_recv,
    load,
    h_send,
    h_recv,
    z_send,
    z_recv,
    z_local,
):
    me, z, sib, dx, dy = place()
    rows, hidden, down_rows, toks = g13.shape[0], g13.shape[1] // 2, g2.shape[0], out_x.shape[1]
    enter(me, z, depth, (sib, me + dx, me + dy), [(z + d) % depth for d in range(1, depth)])
    shift = (0, dx, dy, dx + dy)

    def part(k, block):
        return piece_at(k, p13, p2, block, rows, down_rows, hidden)

    def slot(wide, narrow, j, k):
        half, i = k // 3, k % 3
        return narrow.at[j, half] if i == 2 else wide.at[j, 2 * half + i]

    def hopped(kind, k):
        i = k % 3
        return hop_d.at[kind] if i == 2 else hop_w.at[kind, i]

    order = [(3, k) for k in (0, 3, 1, 4, 2, 5)]
    order += [(1, 0), (2, 3), (1, 1), (2, 4), (1, 2), (2, 5)]
    order += [(2, 0), (1, 3), (2, 1), (1, 4), (2, 2), (1, 5)]
    order += [(0, k) for k in (0, 3, 1, 4, 2, 5)]
    pair, loads = {}, {}
    for j, k in order:
        pair[j, k] = remote(
            part(k, sib + shift[j]),
            slot(sib_w, sib_d, j, k),
            s_send.at[j, k],
            s_recv.at[j, k],
            (sib, z),
        )
        pair[j, k].start()
        loads[j, k] = pltpu.make_async_copy(
            part(k, me + shift[j]), slot(own_w, own_d, j, k), load.at[j, k]
        )
        loads[j, k].start()

    zcopies = []
    for d in range(1, depth):
        to = (z + d) % depth
        block = pl.ds(pl.multiple_of(to * toks, 16), toks)
        for n, (src, dst) in enumerate(((xr, out_x), (q, out_q))):
            copy = remote(
                src.at[block], dst.at[z], z_send.at[d - 1, n], z_recv.at[d - 1, n], (me, to)
            )
            copy.start()
            zcopies.append(copy)
    mine = pl.ds(pl.multiple_of(z * toks, 16), toks)
    zlocal = [
        pltpu.make_async_copy(src.at[mine], dst.at[z], z_local.at[n])
        for n, (src, dst) in enumerate(((xr, out_x), (q, out_q)))
    ]
    for copy in zlocal:
        copy.start()

    def add(dst, terms):
        def step(i, _):
            at = pl.ds(pl.multiple_of(i * 16, 16), 16)
            total = terms[0][at, :].astype(jnp.float32)
            for term in terms[1:]:
                total = total + term[at, :].astype(jnp.float32)
            dst[at, :] = total.astype(dst.dtype)
            return 0

        lax.fori_loop(0, dst.shape[0] // 16, step, 0)

    hops = {}

    def hop(kind, k, j, peer):
        copy = remote(
            slot(own_w, own_d, j, k),
            hopped(kind, k),
            h_send.at[kind, k % 3],
            h_recv.at[kind, k % 3],
            (peer, z),
        )
        copy.start()
        hops[kind, k % 3] = copy

    def terms_of(j, k):
        loads[j, k].wait()
        pair[j, k].wait_recv()
        return [slot(own_w, own_d, j, k), slot(sib_w, sib_d, j, k)]

    for i in range(3):
        for k, kind, peer in ((A_PIECES[i], 0, me + dx), (B_PIECES[i], 3, me + dy)):
            add(slot(own_w, own_d, 3, k), terms_of(3, k))
            hop(kind, k, 3, peer)
    for i in range(3):
        for k, j, kind, peer in ((A_PIECES[i], 1, 1, me + dx), (B_PIECES[i], 2, 4, me + dy)):
            add(slot(own_w, own_d, j, k), terms_of(j, k))
            hop(kind, k, j, peer)
    for i in range(3):
        for k, j, came, kind, peer in (
            (A_PIECES[i], 2, 0, 5, me + dy),
            (B_PIECES[i], 1, 3, 2, me + dx),
        ):
            terms = terms_of(j, k)
            hops[came, i].wait_recv()
            add(slot(own_w, own_d, j, k), terms + [hopped(came, k)])
            hop(kind, k, j, peer)
    for i in range(3):
        for k, first, last in ((A_PIECES[i], 1, 5), (B_PIECES[i], 4, 2)):
            half, n = k // 3, down_rows // 2
            if i == 2:
                dst = g2.at[pl.ds(half * n, n)]
            else:
                n = rows // 2
                dst = g13.at[pl.ds(i * n, n), pl.ds(half * hidden, hidden)]
            terms = terms_of(0, k)
            hops[first, i].wait_recv()
            hops[last, i].wait_recv()
            add(dst, terms + [hopped(first, k), hopped(last, k)])
    for copy in zcopies:
        copy.wait()
    for copy in zlocal:
        copy.wait()
    for copy in pair.values():
        copy.wait_send()
    for copy in hops.values():
        copy.wait_send()


def block_body(
    layer_input,
    output_grad,
    expert_ids,
    gate_probs,
    gate_weight,
    up_weight,
    down_weight,
    gate_moment,
    up_moment,
    down_moment,
    gate_second,
    up_second,
    down_second,
):
    depth, shards = lax.axis_size("expert"), lax.axis_size("dp")
    toks, width = layer_input.shape
    rows, hidden_units = gate_weight.shape[1:]
    down_rows = down_weight.shape[1]
    bf16, f32 = jnp.bfloat16, jnp.float32
    any_spec = pl.BlockSpec(memory_space=pl.ANY)
    vmem_spec = pl.BlockSpec(memory_space=pltpu.VMEM)
    dma = pltpu.SemaphoreType.DMA

    lanes = jnp.arange(128, dtype=jnp.int32)
    named = expert_ids[:, :, None] == lanes[None, None, :]
    zero = jnp.zeros((), bf16)
    gate_table = jnp.sum(jnp.where(named, gate_probs[:, :, None], zero), axis=1)
    w_shard = jnp.concatenate((gate_weight[0], up_weight[0]), axis=1).astype(bf16)
    w_gate_up, w_down, x_rows, dy_rows, gate_rows = pl.pallas_call(
        functools.partial(gather_kernel, depth),
        out_shape=(
            jax.ShapeDtypeStruct((shards * rows, 2 * hidden_units), bf16),
            jax.ShapeDtypeStruct((shards * down_rows, width), bf16),
            jax.ShapeDtypeStruct((depth * toks, width), bf16),
            jax.ShapeDtypeStruct((depth * toks, width), bf16),
            jax.ShapeDtypeStruct((depth * toks, 128), bf16),
        ),
        in_specs=[any_spec] * 5,
        out_specs=(any_spec,) * 5,
        scratch_shapes=[
            dma((7, 6)),
            dma((8, 6)),
            dma((2, depth - 1, 3)),
            dma((2, depth - 1, 3)),
            dma((9,)),
        ],
        compiler_params=pltpu.CompilerParams(collective_id=0, has_side_effects=True),
    )(layer_input, output_grad, gate_table, w_shard, down_weight[0].astype(bf16))

    expert = lax.axis_index("expert")
    gate = jnp.sum(
        jnp.where(lanes[None, :] == expert, gate_rows.astype(f32), 0.0), axis=1, keepdims=True
    )
    out_scaled = (gate * dy_rows.astype(f32)).astype(bf16)
    pre = jnp.dot(x_rows, w_gate_up, preferred_element_type=f32)
    gate_pre, up_pre = pre[:, :hidden_units], pre[:, hidden_units:]
    sigmoid_gate = jax.nn.sigmoid(gate_pre)
    silu_gate = gate_pre * sigmoid_gate
    hidden = (silu_gate * up_pre).astype(bf16)
    expert_out = jnp.dot(hidden, w_down, preferred_element_type=f32)
    prob_rows = jnp.sum(dy_rows.astype(f32) * expert_out, axis=1, keepdims=True).astype(bf16)
    nt = (((1,), (1,)), ((), ()))
    tn = (((0,), (0,)), ((), ()))
    hidden_grad = lax.dot_general(out_scaled, w_down, nt, preferred_element_type=f32)
    dsilu = sigmoid_gate * (1.0 + gate_pre * (1.0 - sigmoid_gate))
    pre_grad = jnp.concatenate(
        (hidden_grad * up_pre * dsilu, hidden_grad * silu_gate), axis=1
    ).astype(bf16)
    input_rows = lax.dot_general(pre_grad, w_gate_up, nt, preferred_element_type=f32).astype(bf16)
    part_gate_up = lax.dot_general(x_rows, pre_grad, tn, preferred_element_type=f32).astype(bf16)
    part_down = lax.dot_general(hidden, out_scaled, tn, preferred_element_type=f32).astype(bf16)

    half, half_down = rows // 2, down_rows // 2
    vm = pltpu.VMEM
    grad_gate_up, grad_down, back_input, back_prob = pl.pallas_call(
        functools.partial(scatter_kernel, depth),
        out_shape=(
            jax.ShapeDtypeStruct((rows, 2 * hidden_units), f32),
            jax.ShapeDtypeStruct((down_rows, width), f32),
            jax.ShapeDtypeStruct((depth, toks, width), bf16),
            jax.ShapeDtypeStruct((depth, toks, 128), bf16),
        ),
        in_specs=[any_spec] * 4,
        out_specs=(vmem_spec, vmem_spec, any_spec, any_spec),
        scratch_shapes=[
            vm((4, 4, half, hidden_units), bf16),
            vm((4, 2, half_down, width), bf16),
            vm((4, 4, half, hidden_units), bf16),
            vm((4, 2, half_down, width), bf16),
            vm((6, 2, half, hidden_units), bf16),
            vm((6, half_down, width), bf16),
            dma((4, 6)),
            dma((4, 6)),
            dma((4, 6)),
            dma((6, 3)),
            dma((6, 3)),
            dma((depth - 1, 2)),
            dma((depth - 1, 2)),
            dma((2,)),
        ],
        compiler_params=pltpu.CompilerParams(
            collective_id=1, has_side_effects=True, vmem_limit_bytes=56 * 1024 * 1024
        ),
    )(part_gate_up, part_down, input_rows, jnp.broadcast_to(prob_rows, (depth * toks, 128)))

    input_grad = jnp.sum(back_input.astype(f32), axis=0).astype(bf16)
    probs = back_prob[:, :, 0].T
    prob_grad = jnp.sum(
        jnp.where(named[:, :, :depth], probs[:, None, :].astype(f32), 0.0), axis=2
    ).astype(bf16)
    new_gate = adamw(gate_weight, gate_moment, gate_second, grad_gate_up[None, :, :hidden_units])
    new_up = adamw(up_weight, up_moment, up_second, grad_gate_up[None, :, hidden_units:])
    new_down = adamw(down_weight, down_moment, down_second, grad_down[None])
    return (input_grad, prob_grad) + tuple(
        value for trio in zip(new_gate, new_up, new_down) for value in trio
    )


def solution(mesh):
    shape = dict(mesh.shape)
    small = shape["dp"] == 8 and shape["expert"] == 4
    return jax.shard_map(
        block_body if small else body,
        mesh=mesh,
        in_specs=(
            P(("dp", "expert"), None),
            P(("dp", "expert"), None),
            P(("dp", "expert"), None),
            P(("dp", "expert"), None),
            P("expert", "dp", None),
            P("expert", "dp", None),
            P("expert", "dp", None),
            P("expert", "dp", None),
            P("expert", "dp", None),
            P("expert", "dp", None),
            P("expert", "dp", None),
            P("expert", "dp", None),
            P("expert", "dp", None),
        ),
        out_specs=(
            P(("dp", "expert"), None),
            P(("dp", "expert"), None),
            P("expert", "dp", None),
            P("expert", "dp", None),
            P("expert", "dp", None),
            P("expert", "dp", None),
            P("expert", "dp", None),
            P("expert", "dp", None),
            P("expert", "dp", None),
            P("expert", "dp", None),
            P("expert", "dp", None),
        ),
        check_vma=False,
    )
```
